32 devices in a mesh: gx: 4 (over z), gy: 2 (over core), gz: 4 (over y, x).
Axes of the slice: x: 2, y: 2, z: 4, core: 2. Of those that a mesh axis runs over, the one named last changes fastest.
Arguments:
- right_side: float32 [32, 32, 512], P('gx', 'gy', 'gz'), may hold values from -8 to 8
- coefficient: float32 [32, 32, 512], P('gx', 'gy', 'gz'), may hold values from 0.05 to 2
Outputs:
- correction: float32 [32, 32, 512], P('gx', 'gy', 'gz')
The draws below stay inside these ranges and needn't reach their ends.
All inputs are finite; a program needn't handle non-finite values.
Results may differ from the reference program's by a relative error of at most 0.00002.
Values sent between devices are 32-bit elements; how exact they have to be, the bound alone decides.
A program may use at most 64 MiB of HBM per device.

```python
import math
import jax
import jax.numpy as jnp

SWEEPS = 4
NX = 32
NY = 32
NZ = 512


def level_of(key, extent, cuts, low, top_value):
    def one(dim, blocks):
        steps = jax.random.uniform(jax.random.fold_in(jax.random.fold_in(key, 6), dim), (blocks,), jnp.float32, low / len(cuts), top_value / len(cuts))
        return jnp.repeat(jnp.exp(steps), extent[dim] // blocks).reshape((-1,) + (1,) * (len(extent) - dim - 1))

    factor_of = one(*cuts[0])
    for cut in cuts[1:]:
        factor_of = factor_of * one(*cut)
    return factor_of


def centred(key, shape, deviation, limit, shards=(), held_as=jnp.bfloat16):
    factor_of = level_of(key, shape, shards, -0.22, 0.18) if shards else 1.0
    array = jax.random.normal(key, shape, jnp.float32) * deviation * factor_of
    return jnp.minimum(jnp.maximum(array, -limit), limit).astype(held_as)


def setup_inputs(seed: int = 0) -> dict:
    keys = jax.random.split(jax.random.key(seed), 3)
    return {
        "right_side": centred(keys[0], (NX, NY, NZ), 3.0, 8.0, ((0, 4), (1, 2), (2, 4)), jnp.float32),
        "coefficient": jnp.clip(jnp.exp(math.log(2.0) - 3.6888794 * jax.random.uniform(keys[1], (NX, NY, NZ), jnp.float32) ** level_of(keys[1], (NX, NY, NZ), ((0, 4), (1, 2), (2, 4)), -0.2, 0.2)), 0.05, 2.0),
    }


RELAX_WEIGHT = 0.8


def restrict(values):
    return values.reshape(values.shape[0] // 2, 2, values.shape[1] // 2, 2, values.shape[2] // 2, 2).mean(axis=(1, 3, 5))


def prolong(values):
    return jnp.repeat(jnp.repeat(jnp.repeat(values, 2, axis=0), 2, axis=1), 2, axis=2)


def neighbours(padded):
    beside_all = padded[2:, 1:-1, 1:-1] + padded[:-2, 1:-1, 1:-1]
    beside_all = beside_all + padded[1:-1, 2:, 1:-1] + padded[1:-1, :-2, 1:-1]
    return beside_all + padded[1:-1, 1:-1, 2:] + padded[1:-1, 1:-1, :-2]


def smooth(residual, coefficient, spacing_scale):
    diagonal = 6.0 * spacing_scale + coefficient
    iterate = RELAX_WEIGHT * residual / diagonal
    for repeat in range(SWEEPS - 1):
        beside_all = neighbours(jnp.pad(iterate, 1))
        iterate = iterate + RELAX_WEIGHT * (residual - (diagonal * iterate - spacing_scale * beside_all)) / diagonal
    return iterate


def plane_term(residual, coefficient):
    return jnp.mean(residual, axis=(0, 1)) / jnp.mean(coefficient + 0.0625, axis=(0, 1))


def reference(right_side, coefficient):
    residual_one = restrict(right_side)
    coeff_one = restrict(coefficient)
    residual_two = restrict(residual_one)
    coeff_two = restrict(coeff_one)
    correction_two = smooth(residual_two, coeff_two, 0.0625) + plane_term(residual_two, coeff_two)[None, None, :]
    correction_one = smooth(residual_one, coeff_one, 0.25) + prolong(correction_two)
    return smooth(right_side, coefficient, 1.0) + prolong(correction_one)
```

```python
import functools
import itertools

import jax
import jax.numpy as jnp
from jax import lax
from jax.experimental import pallas as pl
from jax.experimental.pallas import tpu as pltpu
from jax.sharding import PartitionSpec as P

SWEEPS = 4
RELAX_WEIGHT = 0.8
RIM = SWEEPS - 1

MESH = pl.DeviceIdType.MESH
LANES = 128
ROWS = 8
F32 = jnp.float32

MSG_TILES = 6
MSG_FINE = 2
MSG_TWO = 3
MSG_ONE = (0, 1, 4, 5)
MSG_SPAN = {-1: (0, 4), 0: (0, 6), 1: (2, 6)}


def dot(a, b):
    return jnp.dot(a, b, precision=lax.Precision.HIGHEST, preferred_element_type=F32)


def iota(shape, dim):
    return lax.broadcasted_iota(jnp.int32, shape, dim)


def lane_roll(values, shift):
    shift = shift % LANES
    return values if shift == 0 else pltpu.roll(values, shift, axis=values.ndim - 1)


def row_roll(values, shift):
    axis = values.ndim - 2
    return pltpu.roll(values, shift % values.shape[axis], axis=axis)


def terms(residual, coefficient, scale, mask):
    weight = RELAX_WEIGHT / (6.0 * scale + coefficient)
    return (
        jnp.where(mask, weight * residual, 0.0),
        jnp.where(mask, scale * weight, 0.0),
    )


def sweep_one_column(start, gain):
    value = start
    for _ in range(SWEEPS - 1):
        centre = value[1:-1]
        beside = value[2:] + value[:-2]
        beside = beside + (row_roll(centre, 1) + row_roll(centre, -1))
        beside = beside + (lane_roll(centre, 1) + lane_roll(centre, -1))
        start, gain = start[1:-1], gain[1:-1]
        value = (1.0 - RELAX_WEIGHT) * centre + start + gain * beside
    return value


def kernel(
    counts, extent, right_ref, coeff_ref, out_ref,
    fine, one, group, msg, zbox, pairs,
    load_sem, send_near, recv_near, send_one, recv_one, send_z, recv_z, send_two, recv_two,
):
    count_x, count_y, count_z = counts
    lx, ly, lz = extent
    x1 = lx // 2
    half = lz // 2
    quarter = lz // 4
    spot_x, spot_y, spot_z = (lax.axis_index(a) for a in ("gx", "gy", "gz"))

    def inside(dx, dy, dz):
        ok = None
        for spot, step, count in ((spot_x, dx, count_x), (spot_y, dy, count_y), (spot_z, dz, count_z)):
            if step == 0:
                continue
            here = (spot + step >= 0) & (spot + step < count)
            ok = here if ok is None else ok & here
        return ok

    near = [d for d in itertools.product((-1, 0, 1), repeat=2) if d != (0, 0)]
    along_z = [(dx, dy, dz) for dz in (-1, 1) for dx, dy in itertools.product((0, -1, 1), repeat=2)]
    peers = [p for p in itertools.product(range(count_x), range(count_y)) if p != (0, 0)]

    def target(dx, dy, dz):
        return (spot_x + dx, spot_y + dy, spot_z + dz)

    def peer_id(px, py):
        return (lax.rem(spot_x + px, count_x), lax.rem(spot_y + py, count_y), spot_z)

    barrier = pltpu.get_barrier_semaphore()
    for p in peers:
        pl.semaphore_signal(barrier, inc=1, device_id=peer_id(*p), device_id_type=MESH)
    expected = jnp.int32(len(peers))
    for d in along_z:
        ok = inside(*d)

        @pl.when(ok)
        def _(d=d):
            pl.semaphore_signal(barrier, inc=1, device_id=target(*d), device_id_type=MESH)

        expected = expected + ok.astype(jnp.int32)

    own = (slice(None), pl.ds(RIM, lx), pl.ds(ROWS, ly))
    loads = [
        pltpu.make_async_copy(ref, fine.at[i, pl.ds(RIM, lx), pl.ds(ROWS, ly)], load_sem.at[i])
        for i, ref in enumerate((right_ref, coeff_ref))
    ]
    for copy in loads:
        copy.start()
    for copy in loads:
        copy.wait()

    sums = []
    for i in range(2):
        planes = []
        for x in range(x1):
            total = None
            for a, b in itertools.product(range(2), range(2)):
                part = fine[i, RIM + 2 * x + a, pl.ds(ROWS + b, ly // 2, stride=2), :]
                total = part if total is None else total + part
            planes.append(total)
        for x in range(x1 // 2):
            pairs[i, pl.ds(x * ROWS, ROWS), :] = planes[2 * x] + planes[2 * x + 1]
        twos = pairs[i, pl.ds(0, ROWS, stride=2), :] + pairs[i, pl.ds(1, ROWS, stride=2), :]
        sums.append(jnp.concatenate(planes + [twos], axis=0))
    stacked = jnp.concatenate(sums, axis=1)
    shape = (2 * LANES, LANES)
    to_one = jnp.where(iota(shape, 1) == iota(shape, 0) // 2, 0.125, 0.0).astype(F32)
    to_two = jnp.where(iota(shape, 1) % (2 * quarter) == iota(shape, 0) // 4, 1.0 / 64, 0.0).astype(F32)
    coarse = dot(stacked, jnp.concatenate([to_one, to_two], axis=1))
    own_one = [coarse[x * ROWS:(x + 1) * ROWS, :LANES] for x in range(x1)]
    own_two = coarse[x1 * ROWS:, LANES:]
    my_slot = spot_x * count_y + spot_y
    group[my_slot] = own_two
    for x in range(x1):
        one[RIM + x, ROWS:2 * ROWS, :] = own_one[x]

    lane = iota((ROWS, LANES), 1)
    row = iota((ROWS, LANES), 0)
    place = lane % 8
    tiles_y = ly // ROWS
    pack_r = pack_c = None
    for k in range(lx * tiles_y):
        x, t = divmod(k, tiles_y)
        r = lane_roll(fine[0, RIM + x, pl.ds(ROWS * (1 + t), ROWS), :], 8 * k + 3)
        c = lane_roll(fine[1, RIM + x, pl.ds(ROWS * (1 + t), ROWS), :], 8 * k + 6)
        if pack_r is None:
            pack_r, pack_c = r, c
        else:
            pack_r = jnp.where(lane // 8 == k, r, pack_r)
            pack_c = jnp.where((lane + (LANES - 3)) % LANES // 8 == k, c, pack_c)
    high = jnp.where(place < 3, pack_r, pack_c)
    low = jnp.where((place >= 3) & (place < 6), pack_r, pack_c)
    for side, rim in enumerate((high, low)):
        msg[side, MSG_FINE] = rim
        msg[side, MSG_TWO] = own_two
        for x in range(x1):
            msg[side, MSG_ONE[x]] = own_one[x]

    pl.semaphore_wait(barrier, expected)

    flights = []

    def rim_range(step, size, rim, before):
        if step == 0:
            return pl.ds(before, size), pl.ds(before, size)
        if step < 0:
            return pl.ds(before, rim), pl.ds(before + size, rim)
        return pl.ds(before + size - rim, rim), pl.ds(before - rim, rim)

    for dx, dy in near:
        depth = RIM - abs(dy)
        i = (dx + 1) * 3 + dy + 1
        src_x, dst_x = rim_range(dx, lx, depth, RIM)
        src_y, dst_y = rim_range(dy, ly, ROWS, ROWS)
        flights.append((inside(dx, dy, 0), inside(-dx, -dy, 0), pltpu.make_async_remote_copy(
            src_ref=fine.at[:, src_x, src_y], dst_ref=fine.at[:, dst_x, dst_y],
            send_sem=send_near.at[i], recv_sem=recv_near.at[i],
            device_id=target(dx, dy, 0), device_id_type=MESH)))
        src_x, dst_x = rim_range(dx, x1, depth, RIM)
        src_y, dst_y = rim_range(dy, ROWS, ROWS, ROWS)
        flights.append((inside(dx, dy, 0), inside(-dx, -dy, 0), pltpu.make_async_remote_copy(
            src_ref=one.at[src_x, src_y], dst_ref=one.at[dst_x, dst_y],
            send_sem=send_one.at[i], recv_sem=recv_one.at[i],
            device_id=target(dx, dy, 0), device_id_type=MESH)))
    for dx, dy, dz in along_z:
        side = 0 if dz == 1 else 1
        i = (side * 3 + dx + 1) * 3 + dy + 1
        first, last = MSG_SPAN[dx]
        span = pl.ds(first, last - first)
        flights.append((inside(dx, dy, dz), inside(-dx, -dy, -dz), pltpu.make_async_remote_copy(
            src_ref=msg.at[side, span], dst_ref=zbox.at[side, 1 - dx, 1 - dy, span],
            send_sem=send_z.at[i], recv_sem=recv_z.at[i],
            device_id=target(dx, dy, dz), device_id_type=MESH)))
    for i, p in enumerate(peers):
        flights.append((None, None, pltpu.make_async_remote_copy(
            src_ref=group.at[my_slot], dst_ref=group.at[my_slot],
            send_sem=send_two.at[i], recv_sem=recv_two.at[i],
            device_id=peer_id(*p), device_id_type=MESH)))

    def guarded(condition, act):
        if condition is None:
            act()
        else:
            pl.when(condition)(act)

    for to, _, copy in flights:
        guarded(to, copy.start)
    for _, come, copy in flights:
        guarded(come, copy.wait_recv)
    for to, _, copy in flights:
        guarded(to, copy.wait_send)

    def open_side(spot, count, step):
        if step == 0:
            return jnp.bool_(True)
        return (spot + step >= 0) & (spot + step < count)

    def sides(position, low_end, high_start, spot, count):
        below = jnp.where(spot > 0, 0, low_end)
        above = jnp.where(spot < count - 1, 2 ** 20, high_start)
        return (position >= below) & (position < above)

    above_z = jnp.where(spot_z < count_z - 1, 1, 0)
    below_z = jnp.where(spot_z > 0, 1, 0)

    def lane_mask(shape, width, split):
        at = iota(shape, len(shape) - 1)
        allowed = jnp.where(at < width, 1, jnp.where(at < split, above_z, below_z))
        return allowed > 0

    def z_tile(side, dx, dy, tile):
        return zbox[side, dx + 1, dy + 1, tile]

    lower, upper = [], []
    for dx in range(-2, 3):
        tiles = []
        for dy in (-1, 0, 1):
            at = (jnp.clip(spot_x + dx, 0, count_x - 1) * count_y
                  + jnp.clip(spot_y + dy, 0, count_y - 1))
            tile = group[at]
            r, c = tile, lane_roll(tile, -quarter)
            if abs(dx) < 2:
                up, down = z_tile(1, dx, dy, MSG_TWO), z_tile(0, dx, dy, MSG_TWO)
                r = jnp.where(lane < quarter, r, lane_roll(jnp.where(lane >= 48, up, down), -quarter))
                c = jnp.where(lane < quarter, c, lane_roll(jnp.where(lane >= 80, up, down), -2 * quarter))
            ok = (spot_x + dx >= 0) & (spot_x + dx < count_x) & open_side(spot_y, count_y, dy)
            mask = lane_mask((ROWS, LANES), quarter, 80) & (jnp.where(ok, 1, 0) > 0)
            tiles.append(terms(r, c, 0.0625, mask))
        for x in range(2):
            lo, up_rows = [], []
            for j in range(2):
                before, mid, after = (t[j] for t in tiles)
                if x == 0:
                    lo.append(jnp.where(row < 4, before, row_roll(mid, 4)))
                    up_rows.append(after)
                else:
                    lo.append(jnp.where(row < 4, row_roll(before, 4), mid))
                    up_rows.append(row_roll(after, 4))
            lower.append(lo)
            upper.append(up_rows)
    start_two, gain_two = (
        jnp.stack([jnp.concatenate([lower[i][j], upper[i][j]], axis=0) for i in range(1, 9)])
        for j in range(2)
    )
    value_two = sweep_one_column(start_two, gain_two)[:, :ROWS]
    value_two = jnp.where(row < 4, row_roll(value_two[0], 4), value_two[1])
    total = group[0]
    for i in range(1, count_x * count_y):
        total = total + group[i]
    total = jnp.sum(total, axis=0, keepdims=True) * (1.0 / (count_x * count_y * ROWS))
    plane = total / (lane_roll(jnp.broadcast_to(total, (ROWS, LANES)), -quarter) + 0.0625)
    value_two = jnp.where(lane < quarter, value_two + plane, 0.0)

    empty = one[0, 0:ROWS, :]
    ups, downs = [], []
    for xe in range(x1 + 2 * RIM):
        x = xe - RIM
        up, down = [], []
        for dy in (-1, 0, 1):
            dx = -1 if x < 0 else (1 if x >= x1 else 0)
            if x < -2 or x >= x1 + 2:
                up.append(empty)
                down.append(empty)
                continue
            tile = MSG_ONE[x - dx * x1]
            up.append(z_tile(1, dx, dy, tile))
            down.append(z_tile(0, dx, dy, tile))
        ups.append(jnp.concatenate(up, axis=0))
        downs.append(jnp.concatenate(down, axis=0))
    up, down = jnp.stack(ups), jnp.stack(downs)
    block = one[...]
    shape = block.shape
    at = iota(shape, 2)
    r = jnp.where(at < half, block, lane_roll(jnp.where(at < 32, up, down), half))
    c = jnp.where(at < half, lane_roll(block, half), jnp.where(at < 96, up, down))
    mask = (
        lane_mask(shape, half, 96)
        & sides(iota(shape, 0), RIM, RIM + x1, spot_x, count_x)
        & sides(iota(shape, 1), ROWS, 2 * ROWS, spot_y, count_y)
    )
    value_one = sweep_one_column(*terms(r, c, 0.25, mask))[:, ROWS:2 * ROWS]
    value_one = jnp.where(iota(value_one.shape, 2) < half, value_one, 0.0)

    spread = jnp.concatenate(
        [value_one.reshape(x1 * ROWS, LANES), lane_roll(value_two, half)], axis=0)
    shape = (LANES, LANES)
    at, to = iota(shape, 0), iota(shape, 1)
    widen = jnp.where((at == to // 2) | (at - half == to // 4), 1.0, 0.0).astype(F32)
    spread = dot(spread, widen)
    shape = (lx * ly, (x1 + 1) * ROWS)
    at, to = iota(shape, 0), iota(shape, 1)
    x, y = at // ly, at % ly
    pick = (to == x // 2 * ROWS + y // 2) | (to - x1 * ROWS == x // 4 * 4 + y // 4)
    coarse_part = dot(jnp.where(pick, 1.0, 0.0).astype(F32), spread).reshape(lx, ly, LANES)

    rim_r, rim_c = [], []
    for xe in range(lx + 2 * RIM):
        x = xe - RIM
        if x < -2 or x >= lx + 2:
            pad = fine[0, xe]
            rim_r.append(pad)
            rim_c.append(pad)
            continue
        dx = -1 if x < 0 else (1 if x >= lx else 0)
        row_r, row_c = [], []
        for dy, t in [(-1, tiles_y - 1)] + [(0, t) for t in range(tiles_y)] + [(1, 0)]:
            k = (x - dx * lx) * tiles_y + t
            up, down = z_tile(1, dx, dy, MSG_FINE), z_tile(0, dx, dy, MSG_FINE)
            row_r.append(lane_roll(jnp.where(place < 3, down, up), -8 * k - 3))
            row_c.append(lane_roll(jnp.where((place >= 3) & (place < 6), down, up), -8 * k - 6))
        rim_r.append(jnp.concatenate(row_r, axis=0))
        rim_c.append(jnp.concatenate(row_c, axis=0))
    shape = (lx + 2 * RIM, ly + 2 * ROWS, LANES)
    mask = (
        sides(iota(shape, 0), RIM, RIM + lx, spot_x, count_x)
        & sides(iota(shape, 1), ROWS, ROWS + ly, spot_y, count_y)
    )
    start, gain = terms(fine[0], fine[1], 1.0, mask)
    start_rim, gain_rim = terms(
        jnp.stack(rim_r), jnp.stack(rim_c), 1.0, mask & lane_mask(shape, 0, 64))
    value, value_rim = start, start_rim
    for step in range(SWEEPS - 1):
        def beside(v):
            centre = v[1:-1]
            return v[2:] + v[:-2] + (row_roll(centre, 1) + row_roll(centre, -1))

        near_main, near_rim = beside(value), beside(value_rim)
        start, gain, value = start[1:-1], gain[1:-1], value[1:-1]
        start_rim, gain_rim, value_rim = start_rim[1:-1], gain_rim[1:-1], value_rim[1:-1]
        at = iota(value.shape, 2)
        right, right_rim = lane_roll(value, -1), lane_roll(value_rim, -1)
        left, left_rim = lane_roll(value, 1), lane_roll(value_rim, 1)
        is_last, is_first = at == LANES - 1, at == 0
        near_main = near_main + jnp.where(is_last, right_rim, right) + jnp.where(is_first, left_rim, left)
        near_rim = near_rim + jnp.where(is_last, right, right_rim) + jnp.where(is_first, left, left_rim)
        value = (1.0 - RELAX_WEIGHT) * value + start + gain * near_main
        value_rim = (1.0 - RELAX_WEIGHT) * value_rim + start_rim + gain_rim * near_rim
    out_ref[...] = value[:, ROWS:ROWS + ly] + coarse_part


def per_device(counts, right_side, coefficient):
    lx, ly, lz = right_side.shape
    assert lx // 4 == 2 and ly == 2 * ROWS and lz == LANES
    slots = counts[0] * counts[1]
    dma = pltpu.SemaphoreType.DMA
    return pl.pallas_call(
        functools.partial(kernel, counts, (lx, ly, lz)),
        out_shape=jax.ShapeDtypeStruct(right_side.shape, F32),
        in_specs=[pl.BlockSpec(memory_space=pl.ANY)] * 2,
        out_specs=pl.BlockSpec(memory_space=pltpu.VMEM),
        scratch_shapes=[
            pltpu.VMEM((2, lx + 2 * RIM, ly + 2 * ROWS, LANES), F32),
            pltpu.VMEM((lx // 2 + 2 * RIM, 3 * ROWS, LANES), F32),
            pltpu.VMEM((slots, ROWS, LANES), F32),
            pltpu.VMEM((2, MSG_TILES, ROWS, LANES), F32),
            pltpu.VMEM((2, 3, 3, MSG_TILES, ROWS, LANES), F32),
            pltpu.VMEM((2, 2 * ROWS, LANES), F32),
            dma((2,)),
            dma((9,)), dma((9,)), dma((9,)), dma((9,)),
            dma((18,)), dma((18,)),
            dma((max(slots - 1, 1),)), dma((max(slots - 1, 1),)),
        ],
        compiler_params=pltpu.CompilerParams(
            collective_id=0, has_side_effects=True, vmem_limit_bytes=32 * 1024 * 1024
        ),
    )(right_side, coefficient)


def solution(mesh):
    spec = P("gx", "gy", "gz")
    counts = tuple(mesh.shape[a] for a in ("gx", "gy", "gz"))
    return jax.shard_map(
        functools.partial(per_device, counts), mesh=mesh, in_specs=(spec, spec), out_specs=spec,
        check_vma=False,
    )
```

```python
import functools
import itertools

import jax
import jax.numpy as jnp
from jax import lax
from jax.experimental import pallas as pl
from jax.experimental.pallas import tpu as pltpu
from jax.sharding import PartitionSpec as P

SWEEPS = 4
RELAX_WEIGHT = 0.8
RIM = SWEEPS - 1

MESH = pl.DeviceIdType.MESH
LANES = 128
ROWS = 8
F32 = jnp.float32

MSG_TILES = 2
MSG_FINE = 0
MSG_COARSE = 1


def dot(a, b):
    return jnp.dot(a, b, precision=lax.Precision.HIGHEST, preferred_element_type=F32)


def iota(shape, dim):
    return lax.broadcasted_iota(jnp.int32, shape, dim)


def lane_roll(values, shift):
    shift = shift % LANES
    return values if shift == 0 else pltpu.roll(values, shift, axis=values.ndim - 1)


def row_roll(values, shift):
    axis = values.ndim - 2
    return pltpu.roll(values, shift % values.shape[axis], axis=axis)


def terms(residual, coefficient, scale, mask):
    weight = RELAX_WEIGHT / (6.0 * scale + coefficient)
    return (
        jnp.where(mask, weight * residual, 0.0),
        jnp.where(mask, scale * weight, 0.0),
    )


def sweep_one_column(start, gain):
    value = start
    for _ in range(SWEEPS - 1):
        centre = value[1:-1]
        beside = value[2:] + value[:-2]
        beside = beside + (row_roll(centre, 1) + row_roll(centre, -1))
        beside = beside + (lane_roll(centre, 1) + lane_roll(centre, -1))
        start, gain = start[1:-1], gain[1:-1]
        value = (1.0 - RELAX_WEIGHT) * centre + start + gain * beside
    return value


def kernel(
    counts, extent, right_ref, coeff_ref, out_ref,
    fine, one, group, msg, zbox, pairs,
    load_sem, send_near, recv_near, send_one, recv_one, send_z, recv_z, send_two, recv_two,
):
    count_x, count_y, count_z = counts
    lx, ly, lz = extent
    x1 = lx // 2
    half = lz // 2
    quarter = lz // 4
    spot_x, spot_y, spot_z = (lax.axis_index(a) for a in ("gx", "gy", "gz"))

    def inside(dx, dy, dz):
        ok = None
        for spot, step, count in ((spot_x, dx, count_x), (spot_y, dy, count_y), (spot_z, dz, count_z)):
            if step == 0:
                continue
            here = (spot + step >= 0) & (spot + step < count)
            ok = here if ok is None else ok & here
        return ok

    near = [d for d in itertools.product((-1, 0, 1), repeat=2) if d != (0, 0)]
    along_z = [(dx, dy, dz) for dz in (-1, 1) for dx, dy in itertools.product((0, -1, 1), repeat=2)]
    peers = [p for p in itertools.product(range(count_x), range(count_y)) if p != (0, 0)]

    def target(dx, dy, dz):
        return (spot_x + dx, spot_y + dy, spot_z + dz)

    def peer_id(px, py):
        return (lax.rem(spot_x + px, count_x), lax.rem(spot_y + py, count_y), spot_z)

    barrier = pltpu.get_barrier_semaphore()
    for p in peers:
        pl.semaphore_signal(barrier, inc=1, device_id=peer_id(*p), device_id_type=MESH)
    expected = jnp.int32(len(peers))
    for d in along_z:
        ok = inside(*d)

        @pl.when(ok)
        def _(d=d):
            pl.semaphore_signal(barrier, inc=1, device_id=target(*d), device_id_type=MESH)

        expected = expected + ok.astype(jnp.int32)

    own = (slice(None), pl.ds(RIM, lx), pl.ds(ROWS, ly))
    loads = [
        pltpu.make_async_copy(ref, fine.at[i, pl.ds(RIM, lx), pl.ds(ROWS, ly)], load_sem.at[i])
        for i, ref in enumerate((right_ref, coeff_ref))
    ]
    for copy in loads:
        copy.start()
    for copy in loads:
        copy.wait()

    sums = []
    for i in range(2):
        planes = []
        for x in range(x1):
            total = None
            for a, b in itertools.product(range(2), range(2)):
                part = fine[i, RIM + 2 * x + a, pl.ds(ROWS + b, ly // 2, stride=2), :]
                total = part if total is None else total + part
            planes.append(total)
        for x in range(x1 // 2):
            pairs[i, pl.ds(x * ROWS, ROWS), :] = planes[2 * x] + planes[2 * x + 1]
        twos = pairs[i, pl.ds(0, ROWS, stride=2), :] + pairs[i, pl.ds(1, ROWS, stride=2), :]
        sums.append(jnp.concatenate(planes + [twos], axis=0))
    stacked = jnp.concatenate(sums, axis=1)
    shape = (2 * LANES, LANES)
    to_one = jnp.where(iota(shape, 1) == iota(shape, 0) // 2, 0.125, 0.0).astype(F32)
    to_two = jnp.where(iota(shape, 1) % (2 * quarter) == iota(shape, 0) // 4, 1.0 / 64, 0.0).astype(F32)
    coarse = dot(stacked, jnp.concatenate([to_one, to_two], axis=1))
    own_one = [coarse[x * ROWS:(x + 1) * ROWS, :LANES] for x in range(x1)]
    own_two = coarse[x1 * ROWS:, LANES:]
    my_slot = spot_x * count_y + spot_y
    group[my_slot] = own_two
    for x in range(x1):
        one[RIM + x, ROWS:2 * ROWS, :] = own_one[x]

    lane = iota((ROWS, LANES), 1)
    row = iota((ROWS, LANES), 0)
    place = lane % 8
    tiles_y = ly // ROWS
    pack_r = pack_c = None
    for k in range(lx * tiles_y):
        x, t = divmod(k, tiles_y)
        r = lane_roll(fine[0, RIM + x, pl.ds(ROWS * (1 + t), ROWS), :], 8 * k + 3)
        c = lane_roll(fine[1, RIM + x, pl.ds(ROWS * (1 + t), ROWS), :], 8 * k + 6)
        if pack_r is None:
            pack_r, pack_c = r, c
        else:
            pack_r = jnp.where(lane // 8 == k, r, pack_r)
            pack_c = jnp.where((lane + (LANES - 3)) % LANES // 8 == k, c, pack_c)
    high = jnp.where(place < 3, pack_r, pack_c)
    low = jnp.where((place >= 3) & (place < 6), pack_r, pack_c)
    rims = own_one[0]
    for x in range(1, x1):
        rims = jnp.where((lane + 3) % half // 8 == x, lane_roll(own_one[x], 8 * x), rims)
    rims = jnp.where((lane >= 27) & (lane < 61), own_two, rims)
    rims = jnp.where((lane >= 91) & (lane < 125), lane_roll(own_two, quarter), rims)
    for side, rim in enumerate((high, low)):
        msg[side, MSG_FINE] = rim
        msg[side, MSG_COARSE] = rims

    pl.semaphore_wait(barrier, expected)

    flights_fine, flights_one, flights_z, flights_two = [], [], [], []

    def rim_range(step, size, rim, before):
        if step == 0:
            return pl.ds(before, size), pl.ds(before, size)
        if step < 0:
            return pl.ds(before, rim), pl.ds(before + size, rim)
        return pl.ds(before + size - rim, rim), pl.ds(before - rim, rim)

    for dx, dy in near:
        depth = RIM - abs(dy)
        i = (dx + 1) * 3 + dy + 1
        src_x, dst_x = rim_range(dx, lx, depth, RIM)
        src_y, dst_y = rim_range(dy, ly, ROWS, ROWS)
        flights_fine.append((inside(dx, dy, 0), inside(-dx, -dy, 0), pltpu.make_async_remote_copy(
            src_ref=fine.at[:, src_x, src_y], dst_ref=fine.at[:, dst_x, dst_y],
            send_sem=send_near.at[i], recv_sem=recv_near.at[i],
            device_id=target(dx, dy, 0), device_id_type=MESH)))
        src_x, dst_x = rim_range(dx, x1, depth, RIM)
        src_y, dst_y = rim_range(dy, ROWS, ROWS, ROWS)
        flights_one.append((inside(dx, dy, 0), inside(-dx, -dy, 0), pltpu.make_async_remote_copy(
            src_ref=one.at[src_x, src_y], dst_ref=one.at[dst_x, dst_y],
            send_sem=send_one.at[i], recv_sem=recv_one.at[i],
            device_id=target(dx, dy, 0), device_id_type=MESH)))
    for dx, dy, dz in along_z:
        side = 0 if dz == 1 else 1
        i = (side * 3 + dx + 1) * 3 + dy + 1
        flights_z.append((inside(dx, dy, dz), inside(-dx, -dy, -dz), pltpu.make_async_remote_copy(
            src_ref=msg.at[side], dst_ref=zbox.at[side, 1 - dx, 1 - dy],
            send_sem=send_z.at[i], recv_sem=recv_z.at[i],
            device_id=target(dx, dy, dz), device_id_type=MESH)))
    for i, p in enumerate(peers):
        flights_two.append((None, None, pltpu.make_async_remote_copy(
            src_ref=group.at[my_slot], dst_ref=group.at[my_slot],
            send_sem=send_two.at[i], recv_sem=recv_two.at[i],
            device_id=peer_id(*p), device_id_type=MESH)))

    def guarded(condition, act):
        if condition is None:
            act()
        else:
            pl.when(condition)(act)

    def arrive(flights):
        for _, come, copy in flights:
            guarded(come, copy.wait_recv)

    flights_two.reverse()
    flights = flights_two + flights_z + flights_one + flights_fine
    for to, _, copy in flights:
        guarded(to, copy.start)

    def open_side(spot, count, step):
        if step == 0:
            return jnp.bool_(True)
        return (spot + step >= 0) & (spot + step < count)

    def sides(position, low_end, high_start, spot, count):
        below = jnp.where(spot > 0, 0, low_end)
        above = jnp.where(spot < count - 1, 2 ** 20, high_start)
        return (position >= below) & (position < above)

    above_z = jnp.where(spot_z < count_z - 1, 1, 0)
    below_z = jnp.where(spot_z > 0, 1, 0)

    def lane_mask(shape, width, split):
        at = iota(shape, len(shape) - 1)
        allowed = jnp.where(at < width, 1, jnp.where(at < split, above_z, below_z))
        return allowed > 0

    def z_tile(side, dx, dy, tile):
        return zbox[side, dx + 1, dy + 1, tile]

    arrive(flights_two)
    arrive(flights_z)

    lower, upper = [], []
    for dx in range(-2, 3):
        tiles = []
        for dy in (-1, 0, 1):
            at = (jnp.clip(spot_x + dx, 0, count_x - 1) * count_y
                  + jnp.clip(spot_y + dy, 0, count_y - 1))
            tile = group[at]
            r, c = tile, lane_roll(tile, -quarter)
            if abs(dx) < 2:
                up, down = z_tile(1, dx, dy, MSG_COARSE), z_tile(0, dx, dy, MSG_COARSE)
                r_rim = jnp.where(lane < half, lane_roll(up, half), lane_roll(down, -quarter))
                c_rim = jnp.where(lane < half, up, lane_roll(down, quarter))
                r = jnp.where(lane < quarter, r, r_rim)
                c = jnp.where(lane < quarter, c, c_rim)
            ok = (spot_x + dx >= 0) & (spot_x + dx < count_x) & open_side(spot_y, count_y, dy)
            mask = lane_mask((ROWS, LANES), quarter, 80) & (jnp.where(ok, 1, 0) > 0)
            tiles.append(terms(r, c, 0.0625, mask))
        for x in range(2):
            lo, up_rows = [], []
            for j in range(2):
                before, mid, after = (t[j] for t in tiles)
                if x == 0:
                    lo.append(jnp.where(row < 4, before, row_roll(mid, 4)))
                    up_rows.append(after)
                else:
                    lo.append(jnp.where(row < 4, row_roll(before, 4), mid))
                    up_rows.append(row_roll(after, 4))
            lower.append(lo)
            upper.append(up_rows)
    start_two, gain_two = (
        jnp.stack([jnp.concatenate([lower[i][j], upper[i][j]], axis=0) for i in range(1, 9)])
        for j in range(2)
    )
    value_two = sweep_one_column(start_two, gain_two)[:, :ROWS]
    value_two = jnp.where(row < 4, row_roll(value_two[0], 4), value_two[1])
    total = group[0]
    for i in range(1, count_x * count_y):
        total = total + group[i]
    total = jnp.sum(total, axis=0, keepdims=True) * (1.0 / (count_x * count_y * ROWS))
    plane = total / (lane_roll(jnp.broadcast_to(total, (ROWS, LANES)), -quarter) + 0.0625)
    value_two = jnp.where(lane < quarter, value_two + plane, 0.0)

    arrive(flights_one)
    both = {
        (dx, dy): jnp.where(place < 4, z_tile(1, dx, dy, MSG_COARSE), z_tile(0, dx, dy, MSG_COARSE))
        for dx, dy in itertools.product((-1, 0, 1), repeat=2)
    }
    rim_r, rim_c = [], []
    for xe in range(x1 + 2 * RIM):
        x = xe - RIM
        dx = -1 if x < 0 else (1 if x >= x1 else 0)
        at = 8 * (x - dx * x1)
        if x < -2 or x >= x1 + 2:
            rim_r.append(one[xe])
            rim_c.append(one[xe])
            continue
        rim_r.append(jnp.concatenate([lane_roll(both[dx, dy], half - at) for dy in (-1, 0, 1)], axis=0))
        rim_c.append(jnp.concatenate([lane_roll(both[dx, dy], -at) for dy in (-1, 0, 1)], axis=0))
    block = one[...]
    shape = block.shape
    at = iota(shape, 2)
    r = jnp.where(at < half, block, jnp.stack(rim_r))
    c = jnp.where(at < half, lane_roll(block, half), jnp.stack(rim_c))
    mask = (
        lane_mask(shape, half, 96)
        & sides(iota(shape, 0), RIM, RIM + x1, spot_x, count_x)
        & sides(iota(shape, 1), ROWS, 2 * ROWS, spot_y, count_y)
    )
    value_one = sweep_one_column(*terms(r, c, 0.25, mask))[:, ROWS:2 * ROWS]
    value_one = jnp.where(iota(value_one.shape, 2) < half, value_one, 0.0)

    spread = jnp.concatenate(
        [value_one.reshape(x1 * ROWS, LANES), lane_roll(value_two, half)], axis=0)
    shape = (LANES, LANES)
    at, to = iota(shape, 0), iota(shape, 1)
    widen = jnp.where((at == to // 2) | (at - half == to // 4), 1.0, 0.0).astype(F32)
    spread = dot(spread, widen)
    shape = (lx * ly, (x1 + 1) * ROWS)
    at, to = iota(shape, 0), iota(shape, 1)
    x, y = at // ly, at % ly
    pick = (to == x // 2 * ROWS + y // 2) | (to - x1 * ROWS == x // 4 * 4 + y // 4)
    coarse_part = dot(jnp.where(pick, 1.0, 0.0).astype(F32), spread).reshape(lx, ly, LANES)

    arrive(flights_fine)

    rim_r, rim_c = [], []
    for xe in range(lx + 2 * RIM):
        x = xe - RIM
        if x < -2 or x >= lx + 2:
            pad = fine[0, xe]
            rim_r.append(pad)
            rim_c.append(pad)
            continue
        dx = -1 if x < 0 else (1 if x >= lx else 0)
        row_r, row_c = [], []
        for dy, t in [(-1, tiles_y - 1)] + [(0, t) for t in range(tiles_y)] + [(1, 0)]:
            k = (x - dx * lx) * tiles_y + t
            up, down = z_tile(1, dx, dy, MSG_FINE), z_tile(0, dx, dy, MSG_FINE)
            row_r.append(lane_roll(jnp.where(place < 3, down, up), -8 * k - 3))
            row_c.append(lane_roll(jnp.where((place >= 3) & (place < 6), down, up), -8 * k - 6))
        rim_r.append(jnp.concatenate(row_r, axis=0))
        rim_c.append(jnp.concatenate(row_c, axis=0))
    shape = (lx + 2 * RIM, ly + 2 * ROWS, LANES)
    mask = (
        sides(iota(shape, 0), RIM, RIM + lx, spot_x, count_x)
        & sides(iota(shape, 1), ROWS, ROWS + ly, spot_y, count_y)
    )
    start, gain = terms(fine[0], fine[1], 1.0, mask)
    start_rim, gain_rim = terms(
        jnp.stack(rim_r), jnp.stack(rim_c), 1.0, mask & lane_mask(shape, 0, 64))
    value, value_rim = start, start_rim
    for step in range(SWEEPS - 1):
        def beside(v):
            centre = v[1:-1]
            return v[2:] + v[:-2] + (row_roll(centre, 1) + row_roll(centre, -1))

        near_main, near_rim = beside(value), beside(value_rim)
        start, gain, value = start[1:-1], gain[1:-1], value[1:-1]
        start_rim, gain_rim, value_rim = start_rim[1:-1], gain_rim[1:-1], value_rim[1:-1]
        at = iota(value.shape, 2)
        right, right_rim = lane_roll(value, -1), lane_roll(value_rim, -1)
        left, left_rim = lane_roll(value, 1), lane_roll(value_rim, 1)
        is_last, is_first = at == LANES - 1, at == 0
        near_main = near_main + jnp.where(is_last, right_rim, right) + jnp.where(is_first, left_rim, left)
        near_rim = near_rim + jnp.where(is_last, right, right_rim) + jnp.where(is_first, left, left_rim)
        value = (1.0 - RELAX_WEIGHT) * value + start + gain * near_main
        value_rim = (1.0 - RELAX_WEIGHT) * value_rim + start_rim + gain_rim * near_rim
    out_ref[...] = value[:, ROWS:ROWS + ly] + coarse_part
    for to, _, copy in flights:
        guarded(to, copy.wait_send)


def per_device(counts, right_side, coefficient):
    lx, ly, lz = right_side.shape
    assert lx // 4 == 2 and ly == 2 * ROWS and lz == LANES
    slots = counts[0] * counts[1]
    dma = pltpu.SemaphoreType.DMA
    return pl.pallas_call(
        functools.partial(kernel, counts, (lx, ly, lz)),
        out_shape=jax.ShapeDtypeStruct(right_side.shape, F32),
        in_specs=[pl.BlockSpec(memory_space=pltpu.HBM)] * 2,
        out_specs=pl.BlockSpec(memory_space=pltpu.VMEM),
        scratch_shapes=[
            pltpu.VMEM((2, lx + 2 * RIM, ly + 2 * ROWS, LANES), F32),
            pltpu.VMEM((lx // 2 + 2 * RIM, 3 * ROWS, LANES), F32),
            pltpu.VMEM((slots, ROWS, LANES), F32),
            pltpu.VMEM((2, MSG_TILES, ROWS, LANES), F32),
            pltpu.VMEM((2, 3, 3, MSG_TILES, ROWS, LANES), F32),
            pltpu.VMEM((2, 2 * ROWS, LANES), F32),
            dma((2,)),
            dma((9,)), dma((9,)), dma((9,)), dma((9,)),
            dma((18,)), dma((18,)),
            dma((max(slots - 1, 1),)), dma((max(slots - 1, 1),)),
        ],
        compiler_params=pltpu.CompilerParams(
            collective_id=0, has_side_effects=True, vmem_limit_bytes=32 * 1024 * 1024
        ),
    )(right_side, coefficient)


def solution(mesh):
    spec = P("gx", "gy", "gz")
    counts = tuple(mesh.shape[a] for a in ("gx", "gy", "gz"))
    return jax.shard_map(
        functools.partial(per_device, counts), mesh=mesh, in_specs=(spec, spec), out_specs=spec,
        check_vma=False,
    )
```

```python
import functools
import itertools

import jax
import jax.numpy as jnp
from jax import lax
from jax.experimental import pallas as pl
from jax.experimental.pallas import tpu as pltpu
from jax.sharding import PartitionSpec as P

SWEEPS = 4
RELAX_WEIGHT = 0.8
RIM = SWEEPS - 1
REACH = 2

MESH = pl.DeviceIdType.MESH
LANES = 128
ROWS = 8
F32 = jnp.float32

MSG_TILES = 2
MSG_FINE = 0
MSG_COARSE = 1


def dot(a, b):
    return jnp.dot(a, b, precision=lax.Precision.HIGHEST, preferred_element_type=F32)


def iota(shape, dim):
    return lax.broadcasted_iota(jnp.int32, shape, dim)


def lane_roll(values, shift):
    shift = shift % LANES
    return values if shift == 0 else pltpu.roll(values, shift, axis=values.ndim - 1)


def row_roll(values, shift):
    axis = values.ndim - 2
    return pltpu.roll(values, shift % values.shape[axis], axis=axis)


def terms(residual, coefficient, scale, mask):
    weight = RELAX_WEIGHT / (6.0 * scale + coefficient)
    return (
        jnp.where(mask, weight * residual, 0.0),
        jnp.where(mask, scale * weight, 0.0),
    )


def sweep_one_column(start, gain):
    value = start
    for _ in range(SWEEPS - 1):
        centre = value[1:-1]
        beside = value[2:] + value[:-2]
        beside = beside + (row_roll(centre, 1) + row_roll(centre, -1))
        beside = beside + (lane_roll(centre, 1) + lane_roll(centre, -1))
        start, gain = start[1:-1], gain[1:-1]
        value = (1.0 - RELAX_WEIGHT) * centre + start + gain * beside
    return value


def kernel(
    counts, extent, right_ref, coeff_ref, out_ref,
    fine, one, group, msg, zbox, pairs, far,
    load_sem, send_near, recv_near, send_one, recv_one, send_z, recv_z, send_two, recv_two, far_sem,
):
    count_x, count_y, count_z = counts
    lx, ly, lz = extent
    x1 = lx // 2
    half = lz // 2
    quarter = lz // 4
    spot_x, spot_y, spot_z = (lax.axis_index(a) for a in ("gx", "gy", "gz"))

    def inside(dx, dy, dz):
        ok = None
        for spot, step, count in ((spot_x, dx, count_x), (spot_y, dy, count_y), (spot_z, dz, count_z)):
            if step == 0:
                continue
            here = (spot + step >= 0) & (spot + step < count)
            ok = here if ok is None else ok & here
        return ok

    near = [d for d in itertools.product((-1, 0, 1), repeat=2) if d != (0, 0)]
    along_z = [(dx, dy, dz) for dz in (-1, 1) for dx, dy in itertools.product((0, -1, 1), repeat=2)]
    reach = REACH if count_x <= 2 * REACH else count_x - 1
    relayed = count_x > reach + 1
    peers = [
        (dx, dy)
        for dx, dy in itertools.product(range(-reach, reach + 1), range(1 - count_y, count_y))
        if (dx, dy) != (0, 0) and abs(dx) < count_x
    ]

    def target(dx, dy, dz):
        return (spot_x + dx, spot_y + dy, spot_z + dz)

    barrier = pltpu.get_barrier_semaphore()
    greet = {(dx, dy, 0) for dx, dy in near + peers} | set(along_z)
    expected = jnp.int32(0)
    for d in sorted(greet, key=lambda d: (-abs(d[0]) - abs(d[2]), d)):
        if abs(d[1]) >= count_y or abs(d[0]) >= count_x:
            continue
        ok = inside(*d)

        @pl.when(ok)
        def _(d=d):
            pl.semaphore_signal(barrier, inc=1, device_id=target(*d), device_id_type=MESH)

        expected = expected + ok.astype(jnp.int32)
    loads = [
        pltpu.make_async_copy(ref, fine.at[i, pl.ds(RIM, lx), pl.ds(ROWS, ly)], load_sem.at[i])
        for i, ref in enumerate((right_ref, coeff_ref))
    ]
    for copy in loads:
        copy.start()
    for copy in loads:
        copy.wait()

    sums = []
    for i in range(2):
        planes = []
        for x in range(x1):
            total = None
            for a, b in itertools.product(range(2), range(2)):
                part = fine[i, RIM + 2 * x + a, pl.ds(ROWS + b, ly // 2, stride=2), :]
                total = part if total is None else total + part
            planes.append(total)
        for x in range(x1 // 2):
            pairs[i, pl.ds(x * ROWS, ROWS), :] = planes[2 * x] + planes[2 * x + 1]
        twos = pairs[i, pl.ds(0, ROWS, stride=2), :] + pairs[i, pl.ds(1, ROWS, stride=2), :]
        sums.append(jnp.concatenate(planes + [twos], axis=0))
    stacked = jnp.concatenate(sums, axis=1)
    shape = (2 * LANES, LANES)
    to_one = jnp.where(iota(shape, 1) == iota(shape, 0) // 2, 0.125, 0.0).astype(F32)
    to_two = jnp.where(iota(shape, 1) % (2 * quarter) == iota(shape, 0) // 4, 1.0 / 64, 0.0).astype(F32)
    coarse = dot(stacked, jnp.concatenate([to_one, to_two], axis=1))
    own_one = [coarse[x * ROWS:(x + 1) * ROWS, :LANES] for x in range(x1)]
    own_two = coarse[x1 * ROWS:, LANES:]
    my_slot = spot_x * count_y + spot_y
    group[my_slot] = own_two
    for x in range(x1):
        one[RIM + x, ROWS:2 * ROWS, :] = own_one[x]

    lane = iota((ROWS, LANES), 1)
    row = iota((ROWS, LANES), 0)
    place = lane % 8
    tiles_y = ly // ROWS
    pack_r = pack_c = None
    for k in range(lx * tiles_y):
        x, t = divmod(k, tiles_y)
        r = lane_roll(fine[0, RIM + x, pl.ds(ROWS * (1 + t), ROWS), :], 8 * k + 3)
        c = lane_roll(fine[1, RIM + x, pl.ds(ROWS * (1 + t), ROWS), :], 8 * k + 6)
        if pack_r is None:
            pack_r, pack_c = r, c
        else:
            pack_r = jnp.where(lane // 8 == k, r, pack_r)
            pack_c = jnp.where((lane + (LANES - 3)) % LANES // 8 == k, c, pack_c)
    high = jnp.where(place < 3, pack_r, pack_c)
    low = jnp.where((place >= 3) & (place < 6), pack_r, pack_c)
    rims = own_one[0]
    for x in range(1, x1):
        rims = jnp.where((lane + 3) % half // 8 == x, lane_roll(own_one[x], 8 * x), rims)
    rims = jnp.where((lane >= 27) & (lane < 61), own_two, rims)
    rims = jnp.where((lane >= 91) & (lane < 125), lane_roll(own_two, quarter), rims)
    for side, rim in enumerate((high, low)):
        msg[side, MSG_FINE] = rim
        msg[side, MSG_COARSE] = rims

    pl.semaphore_wait(barrier, expected)

    flights_fine, flights_one, flights_z, flights_two = [], [], [], {True: [], False: []}

    def rim_range(step, size, rim, before):
        if step == 0:
            return pl.ds(before, size), pl.ds(before, size)
        if step < 0:
            return pl.ds(before, rim), pl.ds(before + size, rim)
        return pl.ds(before + size - rim, rim), pl.ds(before - rim, rim)

    for dx, dy in near:
        depth = RIM - abs(dy)
        i = (dx + 1) * 3 + dy + 1
        src_x, dst_x = rim_range(dx, lx, depth, RIM)
        src_y, dst_y = rim_range(dy, ly, ROWS, ROWS)
        flights_fine.append((inside(dx, dy, 0), inside(-dx, -dy, 0), pltpu.make_async_remote_copy(
            src_ref=fine.at[:, src_x, src_y], dst_ref=fine.at[:, dst_x, dst_y],
            send_sem=send_near.at[i], recv_sem=recv_near.at[i],
            device_id=target(dx, dy, 0), device_id_type=MESH)))
        src_x, dst_x = rim_range(dx, x1, depth, RIM)
        src_y, dst_y = rim_range(dy, ROWS, ROWS, ROWS)
        flights_one.append((inside(dx, dy, 0), inside(-dx, -dy, 0), pltpu.make_async_remote_copy(
            src_ref=one.at[src_x, src_y], dst_ref=one.at[dst_x, dst_y],
            send_sem=send_one.at[i], recv_sem=recv_one.at[i],
            device_id=target(dx, dy, 0), device_id_type=MESH)))
    for dx, dy, dz in along_z:
        side = 0 if dz == 1 else 1
        i = (side * 3 + dx + 1) * 3 + dy + 1
        flights_z.append((inside(dx, dy, dz), inside(-dx, -dy, -dz), pltpu.make_async_remote_copy(
            src_ref=msg.at[side], dst_ref=zbox.at[side, 1 - dx, 1 - dy],
            send_sem=send_z.at[i], recv_sem=recv_z.at[i],
            device_id=target(dx, dy, dz), device_id_type=MESH)))
    for i, (dx, dy) in enumerate(peers):
        flights_two[abs(dx) == 1].append((inside(dx, dy, 0), inside(-dx, -dy, 0), pltpu.make_async_remote_copy(
            src_ref=group.at[my_slot], dst_ref=group.at[my_slot],
            send_sem=send_two.at[i], recv_sem=recv_two.at[i],
            device_id=target(dx, dy, 0), device_id_type=MESH)))
    is_relay = (spot_x == reach) | (spot_x == count_x - 1 - reach)
    is_end = (spot_x == 0) | (spot_x == count_x - 1)
    relay = pltpu.make_async_remote_copy(
        src_ref=far.at[0], dst_ref=far.at[1], send_sem=far_sem.at[0], recv_sem=far_sem.at[1],
        device_id=(jnp.where(spot_x == reach, 0, count_x - 1), spot_y, spot_z), device_id_type=MESH)

    def guarded(condition, act):
        if condition is None:
            act()
        else:
            pl.when(condition)(act)

    def arrive(flights):
        for _, come, copy in flights:
            guarded(come, copy.wait_recv)

    flights = flights_two[True] + flights_two[False] + flights_z + flights_one + flights_fine
    for to, _, copy in flights:
        guarded(to, copy.start)

    def open_side(spot, count, step):
        if step == 0:
            return jnp.bool_(True)
        return (spot + step >= 0) & (spot + step < count)

    def sides(position, low_end, high_start, spot, count):
        below = jnp.where(spot > 0, 0, low_end)
        above = jnp.where(spot < count - 1, 2 ** 20, high_start)
        return (position >= below) & (position < above)

    above_z = jnp.where(spot_z < count_z - 1, 1, 0)
    below_z = jnp.where(spot_z > 0, 1, 0)

    def lane_mask(shape, width, split):
        at = iota(shape, len(shape) - 1)
        allowed = jnp.where(at < width, 1, jnp.where(at < split, above_z, below_z))
        return allowed > 0

    def z_tile(side, dx, dy, tile):
        return zbox[side, dx + 1, dy + 1, tile]

    arrive(flights_two[True])
    if relayed:
        @pl.when(is_relay)
        def _():
            end = jnp.where(spot_x == reach, count_x - 1, 0) * count_y
            sums = group[end]
            for i in range(1, count_y):
                sums = sums + group[end + i]
            far[0] = sums
            relay.start()

    arrive(flights_two[False])
    arrive(flights_z)

    lower, upper = [], []
    for dx in range(-2, 3):
        tiles = []
        for dy in (-1, 0, 1):
            at = (jnp.clip(spot_x + dx, 0, count_x - 1) * count_y
                  + jnp.clip(spot_y + dy, 0, count_y - 1))
            tile = group[at]
            r, c = tile, lane_roll(tile, -quarter)
            if abs(dx) < 2:
                up, down = z_tile(1, dx, dy, MSG_COARSE), z_tile(0, dx, dy, MSG_COARSE)
                r_rim = jnp.where(lane < half, lane_roll(up, half), lane_roll(down, -quarter))
                c_rim = jnp.where(lane < half, up, lane_roll(down, quarter))
                r = jnp.where(lane < quarter, r, r_rim)
                c = jnp.where(lane < quarter, c, c_rim)
            ok = (spot_x + dx >= 0) & (spot_x + dx < count_x) & open_side(spot_y, count_y, dy)
            mask = lane_mask((ROWS, LANES), quarter, 80) & (jnp.where(ok, 1, 0) > 0)
            tiles.append(terms(r, c, 0.0625, mask))
        for x in range(2):
            lo, up_rows = [], []
            for j in range(2):
                before, mid, after = (t[j] for t in tiles)
                if x == 0:
                    lo.append(jnp.where(row < 4, before, row_roll(mid, 4)))
                    up_rows.append(after)
                else:
                    lo.append(jnp.where(row < 4, row_roll(before, 4), mid))
                    up_rows.append(row_roll(after, 4))
            lower.append(lo)
            upper.append(up_rows)
    start_two, gain_two = (
        jnp.stack([jnp.concatenate([lower[i][j], upper[i][j]], axis=0) for i in range(1, 9)])
        for j in range(2)
    )
    value_two = sweep_one_column(start_two, gain_two)[:, :ROWS]
    value_two = jnp.where(row < 4, row_roll(value_two[0], 4), value_two[1])
    value_two = jnp.where(lane < quarter, value_two, 0.0)

    arrive(flights_one)
    both = {
        (dx, dy): jnp.where(place < 4, z_tile(1, dx, dy, MSG_COARSE), z_tile(0, dx, dy, MSG_COARSE))
        for dx, dy in itertools.product((-1, 0, 1), repeat=2)
    }
    rim_r, rim_c = [], []
    for xe in range(x1 + 2 * RIM):
        x = xe - RIM
        dx = -1 if x < 0 else (1 if x >= x1 else 0)
        at = 8 * (x - dx * x1)
        if x < -2 or x >= x1 + 2:
            rim_r.append(one[xe])
            rim_c.append(one[xe])
            continue
        rim_r.append(jnp.concatenate([lane_roll(both[dx, dy], half - at) for dy in (-1, 0, 1)], axis=0))
        rim_c.append(jnp.concatenate([lane_roll(both[dx, dy], -at) for dy in (-1, 0, 1)], axis=0))
    block = one[...]
    shape = block.shape
    at = iota(shape, 2)
    r = jnp.where(at < half, block, jnp.stack(rim_r))
    c = jnp.where(at < half, lane_roll(block, half), jnp.stack(rim_c))
    mask = (
        lane_mask(shape, half, 96)
        & sides(iota(shape, 0), RIM, RIM + x1, spot_x, count_x)
        & sides(iota(shape, 1), ROWS, 2 * ROWS, spot_y, count_y)
    )
    value_one = sweep_one_column(*terms(r, c, 0.25, mask))[:, ROWS:2 * ROWS]
    value_one = jnp.where(iota(value_one.shape, 2) < half, value_one, 0.0)

    spread = jnp.concatenate(
        [value_one.reshape(x1 * ROWS, LANES), lane_roll(value_two, half)], axis=0)
    shape = (LANES, LANES)
    at, to = iota(shape, 0), iota(shape, 1)
    widen = jnp.where((at == to // 2) | (at - half == to // 4), 1.0, 0.0).astype(F32)
    spread = dot(spread, widen)
    shape = (lx * ly, (x1 + 1) * ROWS)
    at, to = iota(shape, 0), iota(shape, 1)
    x, y = at // ly, at % ly
    pick = (to == x // 2 * ROWS + y // 2) | (to - x1 * ROWS == x // 4 * 4 + y // 4)
    coarse_part = dot(jnp.where(pick, 1.0, 0.0).astype(F32), spread).reshape(lx, ly, LANES)

    arrive(flights_fine)

    rim_r, rim_c = [], []
    for xe in range(lx + 2 * RIM):
        x = xe - RIM
        if x < -2 or x >= lx + 2:
            pad = fine[0, xe]
            rim_r.append(pad)
            rim_c.append(pad)
            continue
        dx = -1 if x < 0 else (1 if x >= lx else 0)
        row_r, row_c = [], []
        for dy, t in [(-1, tiles_y - 1)] + [(0, t) for t in range(tiles_y)] + [(1, 0)]:
            k = (x - dx * lx) * tiles_y + t
            up, down = z_tile(1, dx, dy, MSG_FINE), z_tile(0, dx, dy, MSG_FINE)
            row_r.append(lane_roll(jnp.where(place < 3, down, up), -8 * k - 3))
            row_c.append(lane_roll(jnp.where((place >= 3) & (place < 6), down, up), -8 * k - 6))
        rim_r.append(jnp.concatenate(row_r, axis=0))
        rim_c.append(jnp.concatenate(row_c, axis=0))
    shape = (lx + 2 * RIM, ly + 2 * ROWS, LANES)
    mask = (
        sides(iota(shape, 0), RIM, RIM + lx, spot_x, count_x)
        & sides(iota(shape, 1), ROWS, ROWS + ly, spot_y, count_y)
    )
    start, gain = terms(fine[0], fine[1], 1.0, mask)
    start_rim, gain_rim = terms(
        jnp.stack(rim_r), jnp.stack(rim_c), 1.0, mask & lane_mask(shape, 0, 64))
    value, value_rim = start, start_rim
    for step in range(SWEEPS - 1):
        def beside(v):
            centre = v[1:-1]
            return v[2:] + v[:-2] + (row_roll(centre, 1) + row_roll(centre, -1))

        near_main, near_rim = beside(value), beside(value_rim)
        start, gain, value = start[1:-1], gain[1:-1], value[1:-1]
        start_rim, gain_rim, value_rim = start_rim[1:-1], gain_rim[1:-1], value_rim[1:-1]
        at = iota(value.shape, 2)
        right, right_rim = lane_roll(value, -1), lane_roll(value_rim, -1)
        left, left_rim = lane_roll(value, 1), lane_roll(value_rim, 1)
        is_last, is_first = at == LANES - 1, at == 0
        near_main = near_main + jnp.where(is_last, right_rim, right) + jnp.where(is_first, left_rim, left)
        near_rim = near_rim + jnp.where(is_last, right, right_rim) + jnp.where(is_first, left, left_rim)
        value = (1.0 - RELAX_WEIGHT) * value + start + gain * near_main
        value_rim = (1.0 - RELAX_WEIGHT) * value_rim + start_rim + gain_rim * near_rim
    fine_part = value[:, ROWS:ROWS + ly] + coarse_part

    total = None
    for x in range(count_x):
        part = group[x * count_y]
        for i in range(1, count_y):
            part = part + group[x * count_y + i]
        if relayed:
            part = jnp.where(jnp.abs(spot_x - x) <= reach, part, 0.0)
        total = part if total is None else total + part
    if relayed:
        pl.when(is_end)(relay.wait_recv)
        total = total + jnp.where(is_end, far[1], 0.0)
    total = jnp.sum(total, axis=0, keepdims=True) * (1.0 / (count_x * count_y * ROWS))
    total = jnp.broadcast_to(total, (ROWS, LANES))
    plane = jnp.where(lane < quarter, total / (lane_roll(total, -quarter) + 0.0625), 0.0)
    plane = dot(plane, jnp.where(iota((LANES, LANES), 0) == iota((LANES, LANES), 1) // 4, 1.0, 0.0).astype(F32))
    out_ref[...] = fine_part + plane[0:1][None]
    if relayed:
        pl.when(is_relay)(relay.wait_send)
    for to, _, copy in flights:
        guarded(to, copy.wait_send)


def per_device(counts, right_side, coefficient):
    lx, ly, lz = right_side.shape
    assert lx // 4 == 2 and ly == 2 * ROWS and lz == LANES
    slots = counts[0] * counts[1]
    dma = pltpu.SemaphoreType.DMA
    return pl.pallas_call(
        functools.partial(kernel, counts, (lx, ly, lz)),
        out_shape=jax.ShapeDtypeStruct(right_side.shape, F32),
        in_specs=[pl.BlockSpec(memory_space=pltpu.HBM)] * 2,
        out_specs=pl.BlockSpec(memory_space=pltpu.VMEM),
        scratch_shapes=[
            pltpu.VMEM((2, lx + 2 * RIM, ly + 2 * ROWS, LANES), F32),
            pltpu.VMEM((lx // 2 + 2 * RIM, 3 * ROWS, LANES), F32),
            pltpu.VMEM((slots, ROWS, LANES), F32),
            pltpu.VMEM((2, MSG_TILES, ROWS, LANES), F32),
            pltpu.VMEM((2, 3, 3, MSG_TILES, ROWS, LANES), F32),
            pltpu.VMEM((2, 2 * ROWS, LANES), F32),
            pltpu.VMEM((2, ROWS, LANES), F32),
            dma((2,)),
            dma((9,)), dma((9,)), dma((9,)), dma((9,)),
            dma((18,)), dma((18,)),
            dma((4 * slots,)), dma((4 * slots,)), dma((2,)),
        ],
        compiler_params=pltpu.CompilerParams(
            collective_id=0, has_side_effects=True, vmem_limit_bytes=32 * 1024 * 1024
        ),
    )(right_side, coefficient)


def solution(mesh):
    spec = P("gx", "gy", "gz")
    counts = tuple(mesh.shape[a] for a in ("gx", "gy", "gz"))
    return jax.shard_map(
        functools.partial(per_device, counts), mesh=mesh, in_specs=(spec, spec), out_specs=spec,
        check_vma=False,
    )
```

```python
import functools
import itertools

import jax
import jax.numpy as jnp
from jax import lax
from jax.experimental import pallas as pl
from jax.experimental.pallas import tpu as pltpu
from jax.sharding import PartitionSpec as P

SWEEPS = 4
RELAX_WEIGHT = 0.8
RIM = SWEEPS - 1

MESH = pl.DeviceIdType.MESH
LANES = 128
ROWS = 8
F32 = jnp.float32

MSG_TILES = 2
MSG_FINE = 0
MSG_COARSE = 1


def dot(a, b):
    return jnp.dot(a, b, precision=lax.Precision.HIGHEST, preferred_element_type=F32)


def iota(shape, dim):
    return lax.broadcasted_iota(jnp.int32, shape, dim)


def lane_roll(values, shift):
    shift = shift % LANES
    return values if shift == 0 else pltpu.roll(values, shift, axis=values.ndim - 1)


def row_roll(values, shift):
    axis = values.ndim - 2
    return pltpu.roll(values, shift % values.shape[axis], axis=axis)


def terms(residual, coefficient, scale, mask):
    weight = RELAX_WEIGHT / (6.0 * scale + coefficient)
    return (
        jnp.where(mask, weight * residual, 0.0),
        jnp.where(mask, scale * weight, 0.0),
    )


def sweep_one_column(start, gain):
    value = start
    for _ in range(SWEEPS - 1):
        centre = value[1:-1]
        beside = value[2:] + value[:-2]
        beside = beside + (row_roll(centre, 1) + row_roll(centre, -1))
        beside = beside + (lane_roll(centre, 1) + lane_roll(centre, -1))
        start, gain = start[1:-1], gain[1:-1]
        value = (1.0 - RELAX_WEIGHT) * centre + start + gain * beside
    return value


def kernel(
    counts, extent, right_ref, coeff_ref, out_ref,
    fine, one, group, msg, zbox, pairs,
    load_sem, send_near, recv_near, send_one, recv_one, send_z, recv_z, send_two, recv_two,
):
    count_x, count_y, count_z = counts
    lx, ly, lz = extent
    x1 = lx // 2
    half = lz // 2
    quarter = lz // 4
    spot_x, spot_y, spot_z = (lax.axis_index(a) for a in ("gx", "gy", "gz"))

    def inside(dx, dy, dz):
        ok = None
        for spot, step, count in ((spot_x, dx, count_x), (spot_y, dy, count_y), (spot_z, dz, count_z)):
            if step == 0:
                continue
            here = (spot + step >= 0) & (spot + step < count)
            ok = here if ok is None else ok & here
        return ok

    near = [d for d in itertools.product((-1, 0, 1), repeat=2) if d != (0, 0)]
    along_z = [(dx, dy, dz) for dz in (-1, 1) for dx, dy in itertools.product((0, -1, 1), repeat=2)]
    peers = [p for p in itertools.product(range(count_x), range(count_y)) if p != (0, 0)]

    def target(dx, dy, dz):
        return (spot_x + dx, spot_y + dy, spot_z + dz)

    def peer_id(px, py):
        return (lax.rem(spot_x + px, count_x), lax.rem(spot_y + py, count_y), spot_z)

    barrier = pltpu.get_barrier_semaphore()
    for p in sorted(peers, key=lambda p: -min(p[0], count_x - p[0])):
        pl.semaphore_signal(barrier, inc=1, device_id=peer_id(*p), device_id_type=MESH)
    expected = jnp.int32(len(peers))
    for d in along_z:
        ok = inside(*d)

        @pl.when(ok)
        def _(d=d):
            pl.semaphore_signal(barrier, inc=1, device_id=target(*d), device_id_type=MESH)

        expected = expected + ok.astype(jnp.int32)

    own = (slice(None), pl.ds(RIM, lx), pl.ds(ROWS, ly))
    loads = [
        pltpu.make_async_copy(ref, fine.at[i, pl.ds(RIM, lx), pl.ds(ROWS, ly)], load_sem.at[i])
        for i, ref in enumerate((right_ref, coeff_ref))
    ]
    for copy in loads:
        copy.start()
    for copy in loads:
        copy.wait()

    sums = []
    for i in range(2):
        planes = []
        for x in range(x1):
            total = None
            for a, b in itertools.product(range(2), range(2)):
                part = fine[i, RIM + 2 * x + a, pl.ds(ROWS + b, ly // 2, stride=2), :]
                total = part if total is None else total + part
            planes.append(total)
        for x in range(x1 // 2):
            pairs[i, pl.ds(x * ROWS, ROWS), :] = planes[2 * x] + planes[2 * x + 1]
        twos = pairs[i, pl.ds(0, ROWS, stride=2), :] + pairs[i, pl.ds(1, ROWS, stride=2), :]
        sums.append(jnp.concatenate(planes + [twos], axis=0))
    stacked = jnp.concatenate(sums, axis=1)
    shape = (2 * LANES, LANES)
    to_one = jnp.where(iota(shape, 1) == iota(shape, 0) // 2, 0.125, 0.0).astype(F32)
    to_two = jnp.where(iota(shape, 1) % (2 * quarter) == iota(shape, 0) // 4, 1.0 / 64, 0.0).astype(F32)
    coarse = dot(stacked, jnp.concatenate([to_one, to_two], axis=1))
    own_one = [coarse[x * ROWS:(x + 1) * ROWS, :LANES] for x in range(x1)]
    own_two = coarse[x1 * ROWS:, LANES:]
    my_slot = spot_x * count_y + spot_y
    group[my_slot] = own_two
    for x in range(x1):
        one[RIM + x, ROWS:2 * ROWS, :] = own_one[x]

    lane = iota((ROWS, LANES), 1)
    row = iota((ROWS, LANES), 0)
    place = lane % 8
    tiles_y = ly // ROWS
    pack_r = pack_c = None
    for k in range(lx * tiles_y):
        x, t = divmod(k, tiles_y)
        r = lane_roll(fine[0, RIM + x, pl.ds(ROWS * (1 + t), ROWS), :], 8 * k + 3)
        c = lane_roll(fine[1, RIM + x, pl.ds(ROWS * (1 + t), ROWS), :], 8 * k + 6)
        if pack_r is None:
            pack_r, pack_c = r, c
        else:
            pack_r = jnp.where(lane // 8 == k, r, pack_r)
            pack_c = jnp.where((lane + (LANES - 3)) % LANES // 8 == k, c, pack_c)
    high = jnp.where(place < 3, pack_r, pack_c)
    low = jnp.where((place >= 3) & (place < 6), pack_r, pack_c)
    rims = own_one[0]
    for x in range(1, x1):
        rims = jnp.where((lane + 3) % half // 8 == x, lane_roll(own_one[x], 8 * x), rims)
    rims = jnp.where((lane >= 27) & (lane < 61), own_two, rims)
    rims = jnp.where((lane >= 91) & (lane < 125), lane_roll(own_two, quarter), rims)
    for side, rim in enumerate((high, low)):
        msg[side, MSG_FINE] = rim
        msg[side, MSG_COARSE] = rims

    pl.semaphore_wait(barrier, expected)

    flights_fine, flights_one, flights_z, flights_two = [], [], [], []

    def rim_range(step, size, rim, before):
        if step == 0:
            return pl.ds(before, size), pl.ds(before, size)
        if step < 0:
            return pl.ds(before, rim), pl.ds(before + size, rim)
        return pl.ds(before + size - rim, rim), pl.ds(before - rim, rim)

    for dx, dy in near:
        depth = RIM - abs(dy)
        i = (dx + 1) * 3 + dy + 1
        src_x, dst_x = rim_range(dx, lx, depth, RIM)
        src_y, dst_y = rim_range(dy, ly, ROWS, ROWS)
        flights_fine.append((inside(dx, dy, 0), inside(-dx, -dy, 0), pltpu.make_async_remote_copy(
            src_ref=fine.at[:, src_x, src_y], dst_ref=fine.at[:, dst_x, dst_y],
            send_sem=send_near.at[i], recv_sem=recv_near.at[i],
            device_id=target(dx, dy, 0), device_id_type=MESH)))
        src_x, dst_x = rim_range(dx, x1, depth, RIM)
        src_y, dst_y = rim_range(dy, ROWS, ROWS, ROWS)
        flights_one.append((inside(dx, dy, 0), inside(-dx, -dy, 0), pltpu.make_async_remote_copy(
            src_ref=one.at[src_x, src_y], dst_ref=one.at[dst_x, dst_y],
            send_sem=send_one.at[i], recv_sem=recv_one.at[i],
            device_id=target(dx, dy, 0), device_id_type=MESH)))
    for dx, dy, dz in along_z:
        side = 0 if dz == 1 else 1
        i = (side * 3 + dx + 1) * 3 + dy + 1
        flights_z.append((inside(dx, dy, dz), inside(-dx, -dy, -dz), pltpu.make_async_remote_copy(
            src_ref=msg.at[side], dst_ref=zbox.at[side, 1 - dx, 1 - dy],
            send_sem=send_z.at[i], recv_sem=recv_z.at[i],
            device_id=target(dx, dy, dz), device_id_type=MESH)))
    for i, p in enumerate(peers):
        flights_two.append((None, None, pltpu.make_async_remote_copy(
            src_ref=group.at[my_slot], dst_ref=group.at[my_slot],
            send_sem=send_two.at[i], recv_sem=recv_two.at[i],
            device_id=peer_id(*p), device_id_type=MESH)))

    def guarded(condition, act):
        if condition is None:
            act()
        else:
            pl.when(condition)(act)

    def arrive(flights):
        for _, come, copy in flights:
            guarded(come, copy.wait_recv)

    flights_two.reverse()
    flights = flights_two + flights_z + flights_one + flights_fine
    for to, _, copy in flights:
        guarded(to, copy.start)

    def open_side(spot, count, step):
        if step == 0:
            return jnp.bool_(True)
        return (spot + step >= 0) & (spot + step < count)

    def sides(position, low_end, high_start, spot, count):
        below = jnp.where(spot > 0, 0, low_end)
        above = jnp.where(spot < count - 1, 2 ** 20, high_start)
        return (position >= below) & (position < above)

    above_z = jnp.where(spot_z < count_z - 1, 1, 0)
    below_z = jnp.where(spot_z > 0, 1, 0)

    def lane_mask(shape, width, split):
        at = iota(shape, len(shape) - 1)
        allowed = jnp.where(at < width, 1, jnp.where(at < split, above_z, below_z))
        return allowed > 0

    def z_tile(side, dx, dy, tile):
        return zbox[side, dx + 1, dy + 1, tile]

    arrive(flights_two)
    arrive(flights_z)

    lower, upper = [], []
    for dx in range(-2, 3):
        tiles = []
        for dy in (-1, 0, 1):
            at = (jnp.clip(spot_x + dx, 0, count_x - 1) * count_y
                  + jnp.clip(spot_y + dy, 0, count_y - 1))
            tile = group[at]
            r, c = tile, lane_roll(tile, -quarter)
            if abs(dx) < 2:
                up, down = z_tile(1, dx, dy, MSG_COARSE), z_tile(0, dx, dy, MSG_COARSE)
                r_rim = jnp.where(lane < half, lane_roll(up, half), lane_roll(down, -quarter))
                c_rim = jnp.where(lane < half, up, lane_roll(down, quarter))
                r = jnp.where(lane < quarter, r, r_rim)
                c = jnp.where(lane < quarter, c, c_rim)
            ok = (spot_x + dx >= 0) & (spot_x + dx < count_x) & open_side(spot_y, count_y, dy)
            mask = lane_mask((ROWS, LANES), quarter, 80) & (jnp.where(ok, 1, 0) > 0)
            tiles.append(terms(r, c, 0.0625, mask))
        for x in range(2):
            lo, up_rows = [], []
            for j in range(2):
                before, mid, after = (t[j] for t in tiles)
                if x == 0:
                    lo.append(jnp.where(row < 4, before, row_roll(mid, 4)))
                    up_rows.append(after)
                else:
                    lo.append(jnp.where(row < 4, row_roll(before, 4), mid))
                    up_rows.append(row_roll(after, 4))
            lower.append(lo)
            upper.append(up_rows)
    start_two, gain_two = (
        jnp.stack([jnp.concatenate([lower[i][j], upper[i][j]], axis=0) for i in range(1, 9)])
        for j in range(2)
    )
    value_two = sweep_one_column(start_two, gain_two)[:, :ROWS]
    value_two = jnp.where(row < 4, row_roll(value_two[0], 4), value_two[1])
    total = group[0]
    for i in range(1, count_x * count_y):
        total = total + group[i]
    total = jnp.sum(total, axis=0, keepdims=True) * (1.0 / (count_x * count_y * ROWS))
    plane = total / (lane_roll(jnp.broadcast_to(total, (ROWS, LANES)), -quarter) + 0.0625)
    value_two = jnp.where(lane < quarter, value_two + plane, 0.0)

    arrive(flights_one)
    both = {
        (dx, dy): jnp.where(place < 4, z_tile(1, dx, dy, MSG_COARSE), z_tile(0, dx, dy, MSG_COARSE))
        for dx, dy in itertools.product((-1, 0, 1), repeat=2)
    }
    rim_r, rim_c = [], []
    for xe in range(x1 + 2 * RIM):
        x = xe - RIM
        dx = -1 if x < 0 else (1 if x >= x1 else 0)
        at = 8 * (x - dx * x1)
        if x < -2 or x >= x1 + 2:
            rim_r.append(one[xe])
            rim_c.append(one[xe])
            continue
        rim_r.append(jnp.concatenate([lane_roll(both[dx, dy], half - at) for dy in (-1, 0, 1)], axis=0))
        rim_c.append(jnp.concatenate([lane_roll(both[dx, dy], -at) for dy in (-1, 0, 1)], axis=0))
    block = one[...]
    shape = block.shape
    at = iota(shape, 2)
    r = jnp.where(at < half, block, jnp.stack(rim_r))
    c = jnp.where(at < half, lane_roll(block, half), jnp.stack(rim_c))
    mask = (
        lane_mask(shape, half, 96)
        & sides(iota(shape, 0), RIM, RIM + x1, spot_x, count_x)
        & sides(iota(shape, 1), ROWS, 2 * ROWS, spot_y, count_y)
    )
    value_one = sweep_one_column(*terms(r, c, 0.25, mask))[:, ROWS:2 * ROWS]
    value_one = jnp.where(iota(value_one.shape, 2) < half, value_one, 0.0)

    spread = jnp.concatenate(
        [value_one.reshape(x1 * ROWS, LANES), lane_roll(value_two, half)], axis=0)
    shape = (LANES, LANES)
    at, to = iota(shape, 0), iota(shape, 1)
    widen = jnp.where((at == to // 2) | (at - half == to // 4), 1.0, 0.0).astype(F32)
    spread = dot(spread, widen)
    shape = (lx * ly, (x1 + 1) * ROWS)
    at, to = iota(shape, 0), iota(shape, 1)
    x, y = at // ly, at % ly
    pick = (to == x // 2 * ROWS + y // 2) | (to - x1 * ROWS == x // 4 * 4 + y // 4)
    coarse_part = dot(jnp.where(pick, 1.0, 0.0).astype(F32), spread).reshape(lx, ly, LANES)

    rim_r, rim_c = [], []
    for xe in range(lx + 2 * RIM):
        x = xe - RIM
        if x < -2 or x >= lx + 2:
            pad = jnp.zeros((ly + 2 * ROWS, LANES), F32)
            rim_r.append(pad)
            rim_c.append(pad)
            continue
        dx = -1 if x < 0 else (1 if x >= lx else 0)
        row_r, row_c = [], []
        for dy, t in [(-1, tiles_y - 1)] + [(0, t) for t in range(tiles_y)] + [(1, 0)]:
            k = (x - dx * lx) * tiles_y + t
            up, down = z_tile(1, dx, dy, MSG_FINE), z_tile(0, dx, dy, MSG_FINE)
            row_r.append(lane_roll(jnp.where(place < 3, down, up), -8 * k - 3))
            row_c.append(lane_roll(jnp.where((place >= 3) & (place < 6), down, up), -8 * k - 6))
        rim_r.append(jnp.concatenate(row_r, axis=0))
        rim_c.append(jnp.concatenate(row_c, axis=0))
    shape = (lx + 2 * RIM, ly + 2 * ROWS, LANES)
    mask = (
        sides(iota(shape, 0), RIM, RIM + lx, spot_x, count_x)
        & sides(iota(shape, 1), ROWS, ROWS + ly, spot_y, count_y)
    )
    start_rim, gain_rim = terms(
        jnp.stack(rim_r), jnp.stack(rim_c), 1.0, mask & lane_mask(shape, 0, 64))
    arrive(flights_fine)
    start, gain = terms(fine[0], fine[1], 1.0, mask)
    value, value_rim = start, start_rim
    for step in range(SWEEPS - 1):
        def beside(v):
            centre = v[1:-1]
            return v[2:] + v[:-2] + (row_roll(centre, 1) + row_roll(centre, -1))

        near_main, near_rim = beside(value), beside(value_rim)
        start, gain, value = start[1:-1], gain[1:-1], value[1:-1]
        start_rim, gain_rim, value_rim = start_rim[1:-1], gain_rim[1:-1], value_rim[1:-1]
        at = iota(value.shape, 2)
        right, right_rim = lane_roll(value, -1), lane_roll(value_rim, -1)
        left, left_rim = lane_roll(value, 1), lane_roll(value_rim, 1)
        is_last, is_first = at == LANES - 1, at == 0
        near_main = near_main + jnp.where(is_last, right_rim, right) + jnp.where(is_first, left_rim, left)
        near_rim = near_rim + jnp.where(is_last, right, right_rim) + jnp.where(is_first, left, left_rim)
        value = (1.0 - RELAX_WEIGHT) * value + start + gain * near_main
        value_rim = (1.0 - RELAX_WEIGHT) * value_rim + start_rim + gain_rim * near_rim
    out_ref[...] = value[:, ROWS:ROWS + ly] + coarse_part
    for to, _, copy in flights:
        guarded(to, copy.wait_send)


def per_device(counts, right_side, coefficient):
    lx, ly, lz = right_side.shape
    assert lx // 4 == 2 and ly == 2 * ROWS and lz == LANES
    slots = counts[0] * counts[1]
    dma = pltpu.SemaphoreType.DMA
    return pl.pallas_call(
        functools.partial(kernel, counts, (lx, ly, lz)),
        out_shape=jax.ShapeDtypeStruct(right_side.shape, F32),
        in_specs=[pl.BlockSpec(memory_space=pltpu.HBM)] * 2,
        out_specs=pl.BlockSpec(memory_space=pltpu.VMEM),
        scratch_shapes=[
            pltpu.VMEM((2, lx + 2 * RIM, ly + 2 * ROWS, LANES), F32),
            pltpu.VMEM((lx // 2 + 2 * RIM, 3 * ROWS, LANES), F32),
            pltpu.VMEM((slots, ROWS, LANES), F32),
            pltpu.VMEM((2, MSG_TILES, ROWS, LANES), F32),
            pltpu.VMEM((2, 3, 3, MSG_TILES, ROWS, LANES), F32),
            pltpu.VMEM((2, 2 * ROWS, LANES), F32),
            dma((2,)),
            dma((9,)), dma((9,)), dma((9,)), dma((9,)),
            dma((18,)), dma((18,)),
            dma((max(slots - 1, 1),)), dma((max(slots - 1, 1),)),
        ],
        compiler_params=pltpu.CompilerParams(
            collective_id=0, has_side_effects=True, vmem_limit_bytes=32 * 1024 * 1024
        ),
    )(right_side, coefficient)


def solution(mesh):
    spec = P("gx", "gy", "gz")
    counts = tuple(mesh.shape[a] for a in ("gx", "gy", "gz"))
    return jax.shard_map(
        functools.partial(per_device, counts), mesh=mesh, in_specs=(spec, spec), out_specs=spec,
        check_vma=False,
    )
```
